128 devices in a mesh: freq: 8 (over z_hi, y), space: 16 (over x, z_lo, core).
Axes of the slice: x: 4, y: 4, z: 4 (z_hi: 2, z_lo: 2; z = z_hi * 2 + z_lo), core: 2. Of those that a mesh axis runs over, the one named last changes fastest.
Arguments:
- traces: float32 [64, 128, 256, 256], P('freq', 'space'), may hold values from -32 to 32
- live: int32 [64, 128, 256], P(None, 'space'), may hold values 0 or 1
Outputs:
- rebuilt: float32 [2, 16, 64, 128, 256], P(None, 'freq', None, 'space')
The draws below stay inside these ranges and needn't reach their ends.
All inputs are finite; a program needn't handle non-finite values. No bound on the sum of `live` on one device may be relied on, other than what follows from the above.
Results may differ from the reference program's by a relative error of at most 0.0003.
Values sent between devices are 32-bit elements; how exact they have to be, the bound alone decides.
No kernel may reach another device: no remote copies, remote signals or barrier semaphores. Data moves between devices by JAX's collectives and lax.ppermute only.
A program may use at most 128 MiB of HBM per device.

```python
import jax
import jax.numpy as jnp
from jax import lax

X = 64
Y = 128
HX = 16
HY = 16
H = 256
NT = 256
F = 16
ITERS = 3


def draw_traces(key, part):
    key = jax.random.fold_in(key, 7)
    first, second = jax.random.split(key, 2)
    position = jnp.arange(Y, dtype=jnp.float32) / (Y - 1.0)
    trend = jnp.exp(jnp.log(3.0) * (position - 0.5)).reshape(1, Y, 1, 1)
    amplitude = jnp.exp(jax.random.uniform(first, (X, Y, H, 1), jnp.float32, jnp.log(0.3), jnp.log(3.0)))
    noise = jnp.clip(jax.random.normal(second, (X, Y, H, NT), jnp.float32), -6.0, 6.0)
    values = noise * amplitude * trend
    return values.astype(jnp.float32)


def set_ends(result, rng, least, high):
    longest = result.shape.index(max(result.shape))
    spots = []
    for shift in (0, 1):
        where = [jax.random.randint(jax.random.fold_in(rng, axis), (), 0, length) for axis, length in enumerate(result.shape)]
        where[longest] = (where[longest] + shift) % result.shape[longest]
        spots.append(tuple(where))
    return result.at[spots[0]].set(least).at[spots[1]].set(high)


def setup_inputs(seed: int = 0) -> dict:
    keys = jax.random.split(jax.random.key(seed), 3)
    traces = draw_traces(jax.random.fold_in(keys[2], 71), 0)
    live = set_ends((jax.random.randint(keys[1], (X, Y, H), 0, 3) < 2).astype(jnp.int32), jax.random.fold_in(keys[1], 1), 0, 1)
    return dict(traces=traces, live=live)


def reference(traces, live):
    def one_row(row):
        return jnp.fft.rfft(row, axis=-1, norm="ortho")[..., 1:F + 1]

    spectra = lax.map(one_row, traces)
    observed = jnp.transpose(spectra, (3, 0, 1, 2)).reshape(F, X, Y, HX, HY)
    weight_live = live.astype(jnp.float32).reshape(1, X, Y, HX, HY)
    observed = observed * weight_live
    field = observed
    for step in range(ITERS):
        tau = 2.0 * 0.5 ** step
        spectrum = jnp.fft.fftn(field, axes=(1, 2, 3, 4), norm="ortho")
        power = jnp.real(spectrum) ** 2 + jnp.imag(spectrum) ** 2
        mean_power = jnp.mean(power, axis=(1, 2, 3, 4), keepdims=True)
        shrunk = spectrum * (power / (power + tau * mean_power + 1e-6))
        recon = jnp.fft.ifftn(shrunk, axes=(1, 2, 3, 4), norm="ortho")
        field = observed + (1.0 - weight_live) * recon
    rebuilt = jnp.stack([jnp.real(field), jnp.imag(field)]).reshape(2, F, X, Y, H)
    return rebuilt.astype(jnp.float32)
```

```python
import functools
import math

import jax
import jax.numpy as jnp
import ml_dtypes
import numpy as np
from jax import lax
from jax.experimental import pallas as pl
from jax.experimental.pallas import tpu as pltpu
from jax.sharding import Mesh, PartitionSpec as P

X = 64
Y = 128
HX = 16
HY = 16
H = 256
NT = 256
F = 16
ITERS = 3
CELLS = float(X * Y * H)
PARTS = 8
TILES = 32
MIB = 1 << 20

AXES = ("zh", "y", "x", "zl", "c")
FREQ = ("zh", "y")
SPACE = ("x", "zl", "c")
SHARE = ("x", "zl")
BF = jnp.bfloat16
F32 = jnp.float32


def split_np(table):
    high = table.astype(ml_dtypes.bfloat16)
    low = (table - high.astype(np.float64)).astype(ml_dtypes.bfloat16)
    return high, low


def time_table():
    times = np.arange(NT)[None, :]
    bins = np.arange(1, F + 1)[:, None]
    angle = 2.0 * np.pi * ((times * bins) % NT) / NT
    rows = np.stack([np.cos(angle), -np.sin(angle)], axis=1) / math.sqrt(NT)
    high, low = split_np(rows.reshape(2 * F, NT))
    return np.concatenate([high, low], axis=0)


def offset_table():
    index = np.arange(H)
    inline, cross = index // HY, index % HY
    phase = (np.outer(inline, inline) * HY + np.outer(cross, cross) * HX) % H
    angle = 2.0 * np.pi * phase / H
    cosine, sine = np.cos(angle), np.sin(angle)
    table = np.block([[cosine, -sine], [sine, cosine]]) / math.sqrt(H * X)
    return np.stack(split_np(table))


def cross_tables():
    part, half, comp, cell = np.meshgrid(
        np.arange(8), np.arange(2), np.arange(2), np.arange(8), indexing="ij"
    )
    cells = (16 * part + 8 * half + cell).reshape(-1)
    comp = comp.reshape(-1)
    waves = np.arange(Y)
    angle = 2.0 * np.pi * (np.outer(waves, cells) % Y) / Y
    cosine, sine = np.cos(angle), np.sin(angle)
    real = np.where(comp == 0, cosine, sine)
    imag = np.where(comp == 0, -sine, cosine)
    forward = np.concatenate([real, imag], axis=0) / math.sqrt(Y)
    inverse = forward.T
    return np.concatenate(split_np(forward)), np.concatenate(split_np(inverse))


def split(value):
    high = value.astype(BF)
    low = (value - high.astype(F32)).astype(BF)
    return high, low


def dot(left, right):
    return lax.dot_general(left, right, (((1,), (0,)), ((), ())), preferred_element_type=F32)


def time_kernel(traces_ref, live_ref, table_ref, out_ref):
    table = table_ref[...]
    rows = []
    for y in range(8):
        high, low = split(traces_ref[0, y])
        dims = (((1,), (1,)), ((), ()))
        both = lax.dot_general(table, high, dims, preferred_element_type=F32)
        rest = lax.dot_general(table[: 2 * F], low, dims, preferred_element_type=F32)
        value = both[: 2 * F] + both[2 * F :] + rest
        rows.append(value)
    stacked = jnp.stack(rows, axis=0)
    turned = jnp.swapaxes(stacked, 0, 1)
    out_ref[:, 0] = turned * live_ref[0][None]


def temporal(traces, live_block, table):
    return pl.pallas_call(
        time_kernel,
        grid=(8,),
        in_specs=[
            pl.BlockSpec((1, 8, H, NT), lambda i: (i, 0, 0, 0)),
            pl.BlockSpec((1, 8, H), lambda i: (i, 0, 0)),
            pl.BlockSpec((4 * F, NT), lambda i: (0, 0)),
        ],
        out_specs=pl.BlockSpec((2 * F, 1, 8, H), lambda i: (0, i, 0, 0)),
        out_shape=jax.ShapeDtypeStruct((2 * F, 8, 8, H), F32),
        compiler_params=pltpu.CompilerParams(vmem_limit_bytes=24 * MIB),
        name="temporal",
    )(traces, live_block, table)


def add(a, b):
    return a[0] + b[0], a[1] + b[1]


def sub(a, b):
    return a[0] - b[0], a[1] - b[1]


def turn(a):
    return a[1], -a[0]


def four(a, b, c, d):
    s, t = add(a, c), sub(a, c)
    u, v = add(b, d), turn(sub(b, d))
    return add(s, u), add(t, v), sub(s, u), sub(t, v)


def eight(values):
    root = math.sqrt(0.5)
    e = four(values[0], values[2], values[4], values[6])
    o = four(values[1], values[3], values[5], values[7])
    o1 = ((o[1][0] + o[1][1]) * root, (o[1][1] - o[1][0]) * root)
    o2 = turn(o[2])
    o3 = ((o[3][1] - o[3][0]) * root, (-o[3][0] - o[3][1]) * root)
    odd = (o[0], o1, o2, o3)
    return [add(e[i], odd[i]) for i in range(4)] + [sub(e[i], odd[i]) for i in range(4)]


def twiddle(value, power):
    power %= 64
    if power == 0:
        return value
    cosine = math.cos(2.0 * math.pi * power / 64)
    sine = math.sin(2.0 * math.pi * power / 64)
    re, im = value
    return re * cosine + im * sine, im * cosine - re * sine


def lines_kernel(stage, *refs):
    refs = list(refs)
    received = refs.pop(0) if stage != "first" else None
    observed = refs.pop(0)
    dead = refs.pop(0) if stage != "first" else None
    table = refs.pop(0)
    out = refs.pop(0)
    one, two = refs.pop(0), refs.pop(0)
    lanes = [pl.ds(0, 128), pl.ds(128, 128)]

    def half(yt, power):
        if stage != "first":
            re = received[:, pl.ds(yt * 16, 8)].reshape(512, H)
            im = received[:, pl.ds(yt * 16 + 8, 8)].reshape(512, H)
            high, low = split(jnp.concatenate([im, re], axis=1))
            result = dot(high, table[0]) + dot(low, table[0]) + dot(high, table[1])
            one[0] = result[:, :H].reshape(8, 8, 8, H)
            one[1] = result[:, H:].reshape(8, 8, 8, H)
            for b in range(8):
                for lane in lanes:
                    values = eight([(one[0, a, b, :, lane], one[1, a, b, :, lane]) for a in range(8)])
                    for d in range(8):
                        re, im = twiddle(values[d], b * d)
                        two[0, d, b, :, lane] = re
                        two[1, d, b, :, lane] = im
        for d in range(8):
            for lane in lanes:
                seen = [
                    (observed[a, yt, 0, d, :, lane], observed[a, yt, 1, d, :, lane]) for a in range(8)
                ]
                if stage == "first":
                    field = seen
                else:
                    back = eight([(two[0, d, b, :, lane], two[1, d, b, :, lane]) for b in range(8)])
                    gone = [dead[yt, a * 8 + d, :, lane] for a in range(8)]
                    field = [
                        (seen[a][0] + gone[a] * back[a][1], seen[a][1] + gone[a] * back[a][0])
                        for a in range(8)
                    ]
                if stage == "last":
                    for a in range(8):
                        out[yt, 0, a * 8 + d, :, lane] = field[a][0]
                        out[yt, 1, a * 8 + d, :, lane] = field[a][1]
                    continue
                for re, im in field:
                    power = power + (re * re + im * im)
                values = eight(field)
                for k in range(8):
                    re, im = twiddle(values[k], d * k)
                    one[0, k, d, :, lane] = re
                    one[1, k, d, :, lane] = im
        if stage == "last":
            return power
        for k in range(8):
            for lane in lanes:
                values = eight([(one[0, k, b, :, lane], one[1, k, b, :, lane]) for b in range(8)])
                for c in range(8):
                    two[0, c, k, :, lane] = values[c][0]
                    two[1, c, k, :, lane] = values[c][1]
        re = two[0].reshape(512, H)
        im = two[1].reshape(512, H)
        high, low = split(jnp.concatenate([re, im], axis=1))
        result = dot(high, table[0]) + dot(low, table[0]) + dot(high, table[1])
        out[:, pl.ds(yt * 16, 8)] = result[:, :H].reshape(8, 8, 8, H)
        out[:, pl.ds(yt * 16 + 8, 8)] = result[:, H:].reshape(8, 8, 8, H)
        return power

    power = lax.fori_loop(0, 2, half, jnp.zeros((8, 128), F32))
    if stage != "last":
        total = jnp.sum(power)
        out[:, TILES] = jnp.full((8, 8, H), total, F32)


def lines(stage, received, observed, dead, table):
    args = [received, observed, dead, table] if stage != "first" else [observed, table]
    if stage == "last":
        shape = (2, 2, X, 8, H)
    else:
        shape = (PARTS, TILES + 1, 8, H)
    vmem = pl.BlockSpec(memory_space=pltpu.VMEM)
    return pl.pallas_call(
        functools.partial(lines_kernel, stage),
        in_specs=[vmem] * len(args),
        out_specs=vmem,
        out_shape=jax.ShapeDtypeStruct(shape, F32),
        scratch_shapes=[pltpu.VMEM((2, 8, 8, 8, H), F32), pltpu.VMEM((2, 8, 8, 8, H), F32)],
        compiler_params=pltpu.CompilerParams(vmem_limit_bytes=32 * MIB),
        name="lines_" + stage,
    )(*args)


def columns_kernel(tau, received, forward, inverse, out):
    total = jnp.sum(received[:, TILES, :, :128]) * (1.0 / 1024.0)
    floor = tau * (total / CELLS) + 1e-06

    def column(kx, carry):
        tiles = []
        for k in range(8):
            for yt in range(2):
                for c in range(2):
                    tiles.append(received[k, yt * 16 + c * 8 + kx])
        high, low = split(jnp.concatenate(tiles, axis=0))
        both = dot(forward[...], high)
        value = both[:256] + both[256:] + dot(forward[:256], low)
        re, im = value[:128], value[128:]
        power = re * re + im * im
        gain = power / (power + floor)
        high, low = split(jnp.concatenate([re * gain, im * gain], axis=0))
        both = dot(inverse[...], high)
        value = both[:256] + both[256:] + dot(inverse[:256], low)
        row = 0
        for k in range(8):
            for yt in range(2):
                for c in range(2):
                    out[k, yt * 16 + c * 8 + kx] = value[row : row + 8]
                    row += 8
        return carry

    lax.fori_loop(0, 8, column, 0)


def columns(tau, received, forward, inverse):
    vmem = pl.BlockSpec(memory_space=pltpu.VMEM)
    return pl.pallas_call(
        functools.partial(columns_kernel, tau),
        in_specs=[vmem] * 3,
        out_specs=vmem,
        out_shape=jax.ShapeDtypeStruct((PARTS, TILES, 8, H), F32),
        compiler_params=pltpu.CompilerParams(vmem_limit_bytes=24 * MIB),
        name="columns",
    )(received, forward, inverse)


def per_device(traces, live):
    core = lax.axis_index("c")
    block = lax.axis_index(FREQ)
    weight = live.astype(F32)
    gone = 1.0 - weight
    other = lax.ppermute(gone, "c", [(0, 1), (1, 0)])
    dead = jnp.where(core == 0, jnp.stack([gone, other]), jnp.stack([other, gone]))
    weight_block = lax.dynamic_slice_in_dim(weight, block * 8, 8, axis=0)
    offsets = jnp.asarray(offset_table())
    forward, inverse = (jnp.asarray(t) for t in cross_tables())

    spectra = temporal(traces, weight_block, jnp.asarray(time_table()))
    spectra = spectra.reshape(F, 2, 8, 8, H)
    observed = lax.all_to_all(spectra, FREQ + ("c",), 0, 0, tiled=True)
    observed = observed.reshape(8, 2, 2, 8, 8, H)

    message = lines("first", None, observed, None, offsets)
    for step in range(ITERS):
        tau = 2.0 * 0.5**step
        whole = lax.all_to_all(message, SHARE, 0, 0, tiled=True)
        shrunk = columns(tau, whole, forward, inverse)
        back = lax.all_to_all(shrunk, SHARE, 0, 0, tiled=True)
        stage = "last" if step == ITERS - 1 else "middle"
        message = lines(stage, back, observed, dead, offsets)
    mine = lax.dynamic_index_in_dim(message, core, 0, keepdims=False)
    yours = lax.dynamic_index_in_dim(message, 1 - core, 0, keepdims=False)
    got = lax.ppermute(yours, "c", [(0, 1), (1, 0)])
    return jnp.where(core == 0, jnp.stack([mine, got], axis=1), jnp.stack([got, mine], axis=1))


def solution(mesh):
    inner = Mesh(mesh.devices.reshape(2, 4, 4, 2, 2), AXES)
    return jax.shard_map(
        per_device,
        mesh=inner,
        in_specs=(P(FREQ, SPACE, None, None), P(None, SPACE, None)),
        out_specs=P(None, FREQ, None, SPACE, None),
        check_vma=False,
    )
```

```python
import functools
import math

import jax
import jax.numpy as jnp
import ml_dtypes
import numpy as np
from jax import lax
from jax.experimental import pallas as pl
from jax.experimental.pallas import tpu as pltpu
from jax.sharding import Mesh, PartitionSpec as P

X = 64
Y = 128
HX = 16
HY = 16
H = 256
NT = 256
F = 16
ITERS = 3
CELLS = float(X * Y * H)
PARTS = 8
TILES = 32
MIB = 1 << 20

AXES = ("zh", "y", "x", "zl", "c")
FREQ = ("zh", "y")
SPACE = ("x", "zl", "c")
SHARE = ("x", "zl")
BF = jnp.bfloat16
F32 = jnp.float32


def split_np(table):
    high = table.astype(ml_dtypes.bfloat16)
    low = (table - high.astype(np.float64)).astype(ml_dtypes.bfloat16)
    return high, low


def time_tables():
    times = np.arange(NT)[None, :]
    bins = np.arange(1, F + 1)[:, None]
    angle = 2.0 * np.pi * ((times * bins) % NT) / NT
    rows = np.stack([np.cos(angle), -np.sin(angle)], axis=1) / math.sqrt(NT)
    rows = rows.reshape(F // 2, 2, 2, NT).transpose(1, 0, 2, 3).reshape(2, F, NT)
    rows = np.stack([rows.reshape(2 * F, NT), rows[::-1].reshape(2 * F, NT)])
    high, low = split_np(rows)
    return np.concatenate([high, low], axis=1)


def block(matrix):
    return np.block([[matrix.real, matrix.imag], [-matrix.imag, matrix.real]])


def offset_tables():
    half = np.arange(HX // 2)
    cross = np.arange(HY)
    inline = np.exp(-2j * np.pi * np.outer(half, half) / (HX // 2))
    turned = np.exp(-2j * np.pi * half / HX)[:, None] * inline
    other = np.exp(-2j * np.pi * np.outer(cross, cross) / HY)
    even, odd = np.kron(inline, other), np.kron(turned, other)
    stack = []
    for matrix in (even, odd, odd.T):
        high, low = split_np(block(matrix) / math.sqrt(H * X))
        stack.append(np.concatenate([high, high, low], axis=0))
    return np.stack(stack)


def cross_tables():
    part, half, comp, cell = np.meshgrid(
        np.arange(8), np.arange(2), np.arange(2), np.arange(8), indexing="ij"
    )
    cells = (16 * part + 8 * half + cell).reshape(-1)
    comp = comp.reshape(-1)
    waves = np.arange(Y)
    angle = 2.0 * np.pi * (np.outer(waves, cells) % Y) / Y
    cosine, sine = np.cos(angle), np.sin(angle)
    real = np.where(comp == 0, cosine, sine)
    imag = np.where(comp == 0, -sine, cosine)
    forward = np.concatenate([real, imag], axis=0) / math.sqrt(Y)
    inverse = forward.T
    return np.concatenate(split_np(forward)), np.concatenate(split_np(inverse))


def split(value):
    high = value.astype(BF)
    low = (value - high.astype(F32)).astype(BF)
    return high, low


def three(left):
    high, low = split(left)
    return jnp.concatenate([high, low, high], axis=1)


def dot(left, right):
    return lax.dot_general(left, right, (((1,), (0,)), ((), ())), preferred_element_type=F32)


def time_kernel(core_ref, traces_hbm, table_hbm, joined, yours, traces, table, sems):
    copies = [pltpu.make_async_copy(table_hbm.at[core_ref[0]], table, sems.at[8])]
    copies += [
        pltpu.make_async_copy(traces_hbm.at[x], traces.at[x], sems.at[x]) for x in range(8)
    ]
    for copy in copies:
        copy.start()
    copies[0].wait()
    dims = (((1,), (1,)), ((), ()))
    for x in range(8):
        copies[1 + x].wait()
        rows = []
        for y in range(8):
            high, low = split(traces[x, y])
            both = lax.dot_general(table[...], high, dims, preferred_element_type=F32)
            rest = lax.dot_general(table[: 2 * F], low, dims, preferred_element_type=F32)
            rows.append(both[: 2 * F] + both[2 * F :] + rest)
        turned = jnp.swapaxes(jnp.stack(rows, axis=0), 0, 1)
        joined[:, 0, :, x] = turned[:F].reshape(8, 2, 8, H)
        yours[:, :, x] = turned[F:].reshape(8, 2, 8, H)


def temporal(core, traces, table):
    anywhere = pl.BlockSpec(memory_space=pl.ANY)
    return pl.pallas_call(
        time_kernel,
        in_specs=[pl.BlockSpec(memory_space=pltpu.SMEM)] + [anywhere] * 2,
        out_specs=[pl.BlockSpec(memory_space=pltpu.VMEM)] * 2,
        out_shape=[
            jax.ShapeDtypeStruct((8, 2, 2, 8, 8, H), F32),
            jax.ShapeDtypeStruct((8, 2, 8, 8, H), F32),
        ],
        scratch_shapes=[
            pltpu.VMEM((8, 8, H, NT), F32),
            pltpu.VMEM((4 * F, NT), BF),
            pltpu.SemaphoreType.DMA((9,)),
        ],
        compiler_params=pltpu.CompilerParams(vmem_limit_bytes=50 * MIB),
        name="temporal",
    )(core, traces, table)


def join_kernel(joined, got, word, live, out):
    del joined, word, live
    out[:, 1] = got[...]


def join(joined, got, word, live):
    vmem = pl.BlockSpec(memory_space=pltpu.VMEM)
    anywhere = pl.BlockSpec(memory_space=pl.ANY)
    return pl.pallas_call(
        join_kernel,
        in_specs=[vmem] * 3 + [anywhere],
        out_specs=vmem,
        out_shape=jax.ShapeDtypeStruct(joined.shape, F32),
        input_output_aliases={0: 0},
        compiler_params=pltpu.CompilerParams(vmem_limit_bytes=8 * MIB),
        name="join",
    )(joined, got, word, live)


def add(a, b):
    return a[0] + b[0], a[1] + b[1]


def sub(a, b):
    return a[0] - b[0], a[1] - b[1]


def turn(a):
    return a[1], -a[0]


def four(a, b, c, d):
    s, t = add(a, c), sub(a, c)
    u, v = add(b, d), turn(sub(b, d))
    return add(s, u), add(t, v), sub(s, u), sub(t, v)


def eight(values):
    root = math.sqrt(0.5)
    e = four(values[0], values[2], values[4], values[6])
    o = four(values[1], values[3], values[5], values[7])
    o1 = ((o[1][0] + o[1][1]) * root, (o[1][1] - o[1][0]) * root)
    o2 = turn(o[2])
    o3 = ((o[3][1] - o[3][0]) * root, (-o[3][0] - o[3][1]) * root)
    odd = (o[0], o1, o2, o3)
    return [add(e[i], odd[i]) for i in range(4)] + [sub(e[i], odd[i]) for i in range(4)]


def twiddle(value, power):
    power %= 64
    if power == 0:
        return value
    cosine = math.cos(2.0 * math.pi * power / 64)
    sine = math.sin(2.0 * math.pi * power / 64)
    re, im = value
    return re * cosine + im * sine, im * cosine - re * sine


def lines_kernel(stage, sides, core_ref, *refs):
    refs = list(refs)
    first, last = stage == "first", stage == "last"
    received = None if first else refs.pop(0)
    observed = refs.pop(0)
    lives = [refs.pop(0) for _ in sides]
    table = refs.pop(0)
    out = refs.pop(0)
    ahead = last and sides[0] == 1
    kept_back = refs.pop(0) if ahead else None
    one, two = refs[:2]
    if last and not ahead:
        held, sent = refs[2:]
        whole, out = out, held
    lanes = [pl.ds(0, 128), pl.ds(128, 128)]
    power = jnp.zeros((8, 128), F32)

    for index, side in enumerate(sides):
        yt = core_ref[0] if side == 0 else 1 - core_ref[0]
        if not first:
            row = 0 if last and not ahead else yt * 16
            re = received[:, pl.ds(row, 8)].reshape(512, H)
            im = received[:, pl.ds(row + 8, 8)].reshape(512, H)
            even = dot(three(jnp.concatenate([im[:, :128], re[:, :128]], axis=1)), table[0])
            odd = dot(three(jnp.concatenate([im[:, 128:], re[:, 128:]], axis=1)), table[2])
            near, far = even + odd, even - odd
            for comp in range(2):
                cut = slice(128 * comp, 128 * comp + 128)
                one[comp, :, :, :, lanes[0]] = near[:, cut].reshape(8, 8, 8, 128)
                one[comp, :, :, :, lanes[1]] = far[:, cut].reshape(8, 8, 8, 128)
            for b in range(8):
                for lane in lanes:
                    values = eight([(one[0, a, b, :, lane], one[1, a, b, :, lane]) for a in range(8)])
                    for d in range(8):
                        re, im = twiddle(values[d], b * d)
                        two[0, d, b, :, lane] = re
                        two[1, d, b, :, lane] = im
        for d in range(8):
            for lane in lanes:
                seen = [
                    (observed[a, side, 0, d, :, lane], observed[a, side, 1, d, :, lane]) for a in range(8)
                ]
                kept = [lives[index][a * 8 + d, :, lane] > 0 for a in range(8)]
                if first:
                    back = [(0.0, 0.0)] * 8
                else:
                    back = eight([(two[0, d, b, :, lane], two[1, d, b, :, lane]) for b in range(8)])
                field = [
                    (jnp.where(kept[a], seen[a][0], back[a][1]), jnp.where(kept[a], seen[a][1], back[a][0]))
                    for a in range(8)
                ]
                if last:
                    for a in range(8):
                        out[0, a * 8 + d, :, lane] = field[a][0]
                        out[1, a * 8 + d, :, lane] = field[a][1]
                    continue
                for re, im in field:
                    power = power + (re * re + im * im)
                values = eight(field)
                for k in range(8):
                    re, im = twiddle(values[k], d * k)
                    one[0, k, d, :, lane] = re
                    one[1, k, d, :, lane] = im
        if last:
            continue
        for k in range(8):
            for lane in lanes:
                values = eight([(one[0, k, b, :, lane], one[1, k, b, :, lane]) for b in range(8)])
                for c in range(8):
                    two[0, c, k, :, lane] = values[c][0]
                    two[1, c, k, :, lane] = values[c][1]
        re = two[0].reshape(512, H)
        im = two[1].reshape(512, H)
        near = jnp.concatenate([re[:, :128] + re[:, 128:], im[:, :128] + im[:, 128:]], axis=1)
        far = jnp.concatenate([re[:, :128] - re[:, 128:], im[:, :128] - im[:, 128:]], axis=1)
        for lane, value in zip(lanes, (dot(three(near), table[0]), dot(three(far), table[1]))):
            out[:, pl.ds(yt * 16, 8), :, lane] = value[:, :128].reshape(8, 8, 8, 128)
            out[:, pl.ds(yt * 16 + 8, 8), :, lane] = value[:, 128:].reshape(8, 8, 8, 128)
    if ahead:
        kept_back[...] = received[:, pl.ds(core_ref[0] * 16, 16)]
    elif last:
        copies = []
        for comp in range(2):
            for part in range(8):
                rows = pl.ds(8 * part, 8)
                copies.append(
                    pltpu.make_async_copy(
                        held.at[comp, rows], whole.at[comp, core_ref[0], rows], sent.at[8 * comp + part]
                    )
                )
        for copy in copies:
            copy.start()
        for copy in copies:
            copy.wait()
    if not last:
        total = jnp.sum(power)
        out[:, TILES] = jnp.full((8, 8, H), total, F32)


def lines(stage, sides, core, received, observed, lives, table):
    vmem = pl.BlockSpec(memory_space=pltpu.VMEM)
    smem = pl.BlockSpec(memory_space=pltpu.SMEM)
    anywhere = pl.BlockSpec(memory_space=pl.ANY)
    scratch = [
        pltpu.VMEM((2, 8, 8, 8, H), F32),
        pltpu.VMEM((2, 8, 8, 8, H), F32),
    ]
    args = [observed, *[lives[side] for side in sides], table]
    specs = [vmem, *[vmem for _ in sides], vmem]
    if stage != "first":
        args, specs = [received] + args, [vmem] + specs
    shapes, out_specs = [(PARTS, TILES + 1, 8, H)], [vmem]
    if stage == "last" and sides[0] == 1:
        shapes, out_specs = [(2, X, 8, H), (PARTS, TILES // 2, 8, H)], [vmem, vmem]
    elif stage == "last":
        shapes, out_specs = [(2, 2, X, 8, H)], [anywhere]
        scratch += [pltpu.VMEM((2, X, 8, H), F32), pltpu.SemaphoreType.DMA((16,))]
    outs = pl.pallas_call(
        functools.partial(lines_kernel, stage, sides),
        in_specs=[smem] + specs,
        out_specs=out_specs,
        out_shape=[jax.ShapeDtypeStruct(shape, F32) for shape in shapes],
        scratch_shapes=scratch,
        compiler_params=pltpu.CompilerParams(vmem_limit_bytes=18 * MIB),
        name="lines_" + stage,
    )(core, *args)
    return outs if len(outs) > 1 else outs[0]


def place_kernel(core_ref, got, rebuilt, out, sems):
    copies = []
    for comp in range(2):
        for part in range(8):
            rows = pl.ds(8 * part, 8)
            copies.append(
                pltpu.make_async_copy(
                    got.at[comp, rows], out.at[comp, 1 - core_ref[0], rows], sems.at[8 * comp + part]
                )
            )
    for copy in copies:
        copy.start()
    for copy in copies:
        copy.wait()


def place(core, got, rebuilt):
    anywhere = pl.BlockSpec(memory_space=pl.ANY)
    return pl.pallas_call(
        place_kernel,
        in_specs=[
            pl.BlockSpec(memory_space=pltpu.SMEM),
            pl.BlockSpec(memory_space=pltpu.VMEM),
            anywhere,
        ],
        out_specs=anywhere,
        out_shape=jax.ShapeDtypeStruct(rebuilt.shape, F32),
        scratch_shapes=[pltpu.SemaphoreType.DMA((16,))],
        input_output_aliases={2: 0},
        compiler_params=pltpu.CompilerParams(vmem_limit_bytes=8 * MIB),
        name="place",
    )(core, got, rebuilt)


def columns_kernel(tau, received, forward, inverse, out):
    total = jnp.sum(received[:, TILES, :, :128]) * (1.0 / 1024.0)
    floor = tau * (total / CELLS) + 1e-06

    def column(kx, carry):
        tiles = []
        for k in range(8):
            for yt in range(2):
                for c in range(2):
                    tiles.append(received[k, yt * 16 + c * 8 + kx])
        high, low = split(jnp.concatenate(tiles, axis=0))
        both = dot(forward[...], high)
        value = both[:256] + both[256:] + dot(forward[:256], low)
        re, im = value[:128], value[128:]
        power = re * re + im * im
        gain = power / (power + floor)
        high, low = split(jnp.concatenate([re * gain, im * gain], axis=0))
        both = dot(inverse[...], high)
        value = both[:256] + both[256:] + dot(inverse[:256], low)
        row = 0
        for k in range(8):
            for yt in range(2):
                for c in range(2):
                    out[k, yt * 16 + c * 8 + kx] = value[row : row + 8]
                    row += 8
        return carry

    lax.fori_loop(0, 8, column, 0, unroll=4)


def columns(tau, received, forward, inverse):
    vmem = pl.BlockSpec(memory_space=pltpu.VMEM)
    return pl.pallas_call(
        functools.partial(columns_kernel, tau),
        in_specs=[vmem] * 3,
        out_specs=vmem,
        out_shape=jax.ShapeDtypeStruct((PARTS, TILES, 8, H), F32),
        compiler_params=pltpu.CompilerParams(vmem_limit_bytes=16 * MIB),
        name="columns",
    )(received, forward, inverse)


def per_device(traces, live):
    core = lax.axis_index("c")[None]
    swap = [(0, 1), (1, 0)]
    lives = [live, lax.ppermute(live, "c", swap)]
    offsets = jnp.asarray(offset_tables())
    forward, inverse = (jnp.asarray(t) for t in cross_tables())

    joined, yours = temporal(core, traces, jnp.asarray(time_tables()))
    got = lax.ppermute(yours, "c", swap)
    ring = [(2 * x, (2 * x + 2) % 8) for x in range(4)]
    word = lax.ppermute(got[0, 0, 0, :, :128], ("x", "c"), ring)
    joined = join(joined, got, word, lives[1])
    observed = lax.all_to_all(joined, FREQ, 0, 0, tiled=True)

    both = (0, 1)
    message = lines("first", both, core, None, observed, lives, offsets)
    for step in range(ITERS):
        tau = 2.0 * 0.5**step
        whole = lax.all_to_all(message, SHARE, 0, 0, tiled=True)
        shrunk = columns(tau, whole, forward, inverse)
        back = lax.all_to_all(shrunk, SHARE, 0, 0, tiled=True)
        if step < ITERS - 1:
            message = lines("middle", both, core, back, observed, lives, offsets)
    yours, back = lines("last", (1,), core, back, observed, lives, offsets)
    got = lax.ppermute(yours, "c", swap)
    rebuilt = lines("last", (0,), core, back, observed, lives, offsets)
    return place(core, got, rebuilt)


def solution(mesh):
    inner = Mesh(mesh.devices.reshape(2, 4, 4, 2, 2), AXES)
    return jax.shard_map(
        per_device,
        mesh=inner,
        in_specs=(P(FREQ, SPACE, None, None), P(None, SPACE, None)),
        out_specs=P(None, FREQ, None, SPACE, None),
        check_vma=False,
    )
```

```python
import functools
import math

import jax
import jax.numpy as jnp
import ml_dtypes
import numpy as np
from jax import lax
from jax.experimental import pallas as pl
from jax.experimental.pallas import tpu as pltpu
from jax.sharding import Mesh, PartitionSpec as P

X = 64
Y = 128
HX = 16
HY = 16
H = 256
NT = 256
F = 16
ITERS = 3
CELLS = float(X * Y * H)
PARTS = 8
TILES = 32
MIB = 1 << 20

AXES = ("zh", "y", "x", "zl", "c")
FREQ = ("zh", "y")
SPACE = ("x", "zl", "c")
SHARE = ("x", "zl")
BF = jnp.bfloat16
F32 = jnp.float32


def split_np(table):
    high = table.astype(ml_dtypes.bfloat16)
    low = (table - high.astype(np.float64)).astype(ml_dtypes.bfloat16)
    return high, low


def time_tables():
    times = np.arange(NT)[None, :]
    bins = np.arange(1, F + 1)[:, None]
    angle = 2.0 * np.pi * ((times * bins) % NT) / NT
    rows = np.stack([np.cos(angle), -np.sin(angle)], axis=1) / math.sqrt(NT)
    rows = rows.reshape(F // 2, 2, 2, NT).transpose(1, 0, 2, 3).reshape(2, F, NT)
    rows = np.stack([rows.reshape(2 * F, NT), rows[::-1].reshape(2 * F, NT)])
    high, low = split_np(rows)
    return np.concatenate([high, low], axis=1)


def block(matrix):
    return np.block([[matrix.real, matrix.imag], [-matrix.imag, matrix.real]])


def offset_tables():
    half = np.arange(HX // 2)
    cross = np.arange(HY)
    inline = np.exp(-2j * np.pi * np.outer(half, half) / (HX // 2))
    turned = np.exp(-2j * np.pi * half / HX)[:, None] * inline
    other = np.exp(-2j * np.pi * np.outer(cross, cross) / HY)
    even, odd = np.kron(inline, other), np.kron(turned, other)
    stack = []
    for matrix in (even, odd, odd.T):
        high, low = split_np(block(matrix) / math.sqrt(H * X))
        stack.append(np.concatenate([high, high, low], axis=0))
    return np.stack(stack)


def cross_tables():
    part, half, comp, cell = np.meshgrid(
        np.arange(8), np.arange(2), np.arange(2), np.arange(8), indexing="ij"
    )
    cells = (16 * part + 8 * half + cell).reshape(-1)
    comp = comp.reshape(-1)
    waves = np.arange(Y)
    angle = 2.0 * np.pi * (np.outer(waves, cells) % Y) / Y
    cosine, sine = np.cos(angle), np.sin(angle)
    real = np.where(comp == 0, cosine, sine)
    imag = np.where(comp == 0, -sine, cosine)
    forward = np.concatenate([real, imag], axis=0) / math.sqrt(Y)
    inverse = forward.T
    return np.concatenate(split_np(forward)), np.concatenate(split_np(inverse))


def split(value):
    high = value.astype(BF)
    low = (value - high.astype(F32)).astype(BF)
    return high, low


def three(left):
    high, low = split(left)
    return jnp.concatenate([high, low, high], axis=1)


def dot(left, right):
    return lax.dot_general(left, right, (((1,), (0,)), ((), ())), preferred_element_type=F32)


def time_kernel(core_ref, traces_hbm, table_hbm, joined, yours, traces, table, sems):
    copies = [pltpu.make_async_copy(table_hbm.at[core_ref[0]], table, sems.at[8])]
    copies += [
        pltpu.make_async_copy(traces_hbm.at[x], traces.at[x], sems.at[x]) for x in range(8)
    ]
    for copy in copies:
        copy.start()
    copies[0].wait()
    dims = (((1,), (1,)), ((), ()))
    for x in range(8):
        copies[1 + x].wait()
        rows = []
        for y in range(8):
            high, low = split(traces[x, y])
            both = lax.dot_general(table[...], high, dims, preferred_element_type=F32)
            rest = lax.dot_general(table[: 2 * F], low, dims, preferred_element_type=F32)
            rows.append(both[: 2 * F] + both[2 * F :] + rest)
        turned = jnp.swapaxes(jnp.stack(rows, axis=0), 0, 1)
        joined[:, 0, :, x] = turned[:F].reshape(8, 2, 8, H)
        yours[:, :, x] = turned[F:].reshape(8, 2, 8, H)


def temporal(core, traces, table):
    anywhere = pl.BlockSpec(memory_space=pl.ANY)
    return pl.pallas_call(
        time_kernel,
        in_specs=[pl.BlockSpec(memory_space=pltpu.SMEM)] + [anywhere] * 2,
        out_specs=[pl.BlockSpec(memory_space=pltpu.VMEM)] * 2,
        out_shape=[
            jax.ShapeDtypeStruct((8, 2, 2, 8, 8, H), F32),
            jax.ShapeDtypeStruct((8, 2, 8, 8, H), F32),
        ],
        scratch_shapes=[
            pltpu.VMEM((8, 8, H, NT), F32),
            pltpu.VMEM((4 * F, NT), BF),
            pltpu.SemaphoreType.DMA((9,)),
        ],
        compiler_params=pltpu.CompilerParams(vmem_limit_bytes=50 * MIB),
        name="temporal",
    )(core, traces, table)


def join_kernel(joined, got, word, live, out):
    del joined, word, live
    out[:, 1] = got[...]


def join(joined, got, word, live):
    vmem = pl.BlockSpec(memory_space=pltpu.VMEM)
    anywhere = pl.BlockSpec(memory_space=pl.ANY)
    return pl.pallas_call(
        join_kernel,
        in_specs=[vmem] * 3 + [anywhere],
        out_specs=vmem,
        out_shape=jax.ShapeDtypeStruct(joined.shape, F32),
        input_output_aliases={0: 0},
        compiler_params=pltpu.CompilerParams(vmem_limit_bytes=8 * MIB),
        name="join",
    )(joined, got, word, live)


def add(a, b):
    return a[0] + b[0], a[1] + b[1]


def sub(a, b):
    return a[0] - b[0], a[1] - b[1]


def turn(a):
    return a[1], -a[0]


def four(a, b, c, d):
    s, t = add(a, c), sub(a, c)
    u, v = add(b, d), turn(sub(b, d))
    return add(s, u), add(t, v), sub(s, u), sub(t, v)


def eight(values):
    root = math.sqrt(0.5)
    e = four(values[0], values[2], values[4], values[6])
    o = four(values[1], values[3], values[5], values[7])
    o1 = ((o[1][0] + o[1][1]) * root, (o[1][1] - o[1][0]) * root)
    o2 = turn(o[2])
    o3 = ((o[3][1] - o[3][0]) * root, (-o[3][0] - o[3][1]) * root)
    odd = (o[0], o1, o2, o3)
    return [add(e[i], odd[i]) for i in range(4)] + [sub(e[i], odd[i]) for i in range(4)]


def twiddle(value, power):
    power %= 64
    if power == 0:
        return value
    cosine = math.cos(2.0 * math.pi * power / 64)
    sine = math.sin(2.0 * math.pi * power / 64)
    re, im = value
    return re * cosine + im * sine, im * cosine - re * sine


def lines_kernel(stage, sides, core_ref, *refs):
    refs = list(refs)
    first, last = stage == "first", stage == "last"
    received = None if first else refs.pop(0)
    observed = refs.pop(0)
    lives = [refs.pop(0) for _ in sides]
    table = refs.pop(0)
    out = refs.pop(0)
    ahead = last and sides[0] == 1
    kept_back = refs.pop(0) if ahead else None
    one, two = refs[:2]
    if last and not ahead:
        held, sent = refs[2:]
        whole, out = out, held
    lanes = [pl.ds(0, 128), pl.ds(128, 128)]
    power = jnp.zeros((8, 128), F32)

    for index, side in enumerate(sides):
        yt = core_ref[0] if side == 0 else 1 - core_ref[0]
        if not first:
            row = 0 if last and not ahead else yt * 16
            re = received[:, pl.ds(row, 8)].reshape(512, H)
            im = received[:, pl.ds(row + 8, 8)].reshape(512, H)
            even = dot(three(jnp.concatenate([im[:, :128], re[:, :128]], axis=1)), table[0])
            odd = dot(three(jnp.concatenate([im[:, 128:], re[:, 128:]], axis=1)), table[2])
            near, far = even + odd, even - odd
            for comp in range(2):
                cut = slice(128 * comp, 128 * comp + 128)
                one[comp, :, :, :, lanes[0]] = near[:, cut].reshape(8, 8, 8, 128)
                one[comp, :, :, :, lanes[1]] = far[:, cut].reshape(8, 8, 8, 128)
            for b in range(8):
                for lane in lanes:
                    values = eight([(one[0, a, b, :, lane], one[1, a, b, :, lane]) for a in range(8)])
                    for d in range(8):
                        re, im = twiddle(values[d], b * d)
                        two[0, d, b, :, lane] = re
                        two[1, d, b, :, lane] = im
        for d in range(8):
            for lane in lanes:
                seen = [
                    (observed[a, side, 0, d, :, lane], observed[a, side, 1, d, :, lane]) for a in range(8)
                ]
                kept = [lives[index][a * 8 + d, :, lane] > 0 for a in range(8)]
                if first:
                    back = [(0.0, 0.0)] * 8
                else:
                    back = eight([(two[0, d, b, :, lane], two[1, d, b, :, lane]) for b in range(8)])
                field = [
                    (jnp.where(kept[a], seen[a][0], back[a][1]), jnp.where(kept[a], seen[a][1], back[a][0]))
                    for a in range(8)
                ]
                if last:
                    for a in range(8):
                        out[0, a * 8 + d, :, lane] = field[a][0]
                        out[1, a * 8 + d, :, lane] = field[a][1]
                    continue
                for re, im in field:
                    power = power + (re * re + im * im)
                values = eight(field)
                for k in range(8):
                    re, im = twiddle(values[k], d * k)
                    one[0, k, d, :, lane] = re
                    one[1, k, d, :, lane] = im
        if last:
            continue
        for k in range(8):
            for lane in lanes:
                values = eight([(one[0, k, b, :, lane], one[1, k, b, :, lane]) for b in range(8)])
                for c in range(8):
                    two[0, c, k, :, lane] = values[c][0]
                    two[1, c, k, :, lane] = values[c][1]
        re = two[0].reshape(512, H)
        im = two[1].reshape(512, H)
        near = jnp.concatenate([re[:, :128] + re[:, 128:], im[:, :128] + im[:, 128:]], axis=1)
        far = jnp.concatenate([re[:, :128] - re[:, 128:], im[:, :128] - im[:, 128:]], axis=1)
        for lane, value in zip(lanes, (dot(three(near), table[0]), dot(three(far), table[1]))):
            out[:, pl.ds(yt * 16, 8), :, lane] = value[:, :128].reshape(8, 8, 8, 128)
            out[:, pl.ds(yt * 16 + 8, 8), :, lane] = value[:, 128:].reshape(8, 8, 8, 128)
    if ahead:
        kept_back[...] = received[:, pl.ds(core_ref[0] * 16, 16)]
    elif last:
        copies = []
        for comp in range(2):
            for part in range(8):
                rows = pl.ds(8 * part, 8)
                copies.append(
                    pltpu.make_async_copy(
                        held.at[comp, rows], whole.at[comp, core_ref[0], rows], sent.at[8 * comp + part]
                    )
                )
        for copy in copies:
            copy.start()
        for copy in copies:
            copy.wait()
    if not last:
        total = jnp.sum(power)
        out[:, TILES] = jnp.full((8, 8, H), total, F32)


def lines(stage, sides, core, received, observed, lives, table):
    vmem = pl.BlockSpec(memory_space=pltpu.VMEM)
    smem = pl.BlockSpec(memory_space=pltpu.SMEM)
    anywhere = pl.BlockSpec(memory_space=pl.ANY)
    scratch = [
        pltpu.VMEM((2, 8, 8, 8, H), F32),
        pltpu.VMEM((2, 8, 8, 8, H), F32),
    ]
    args = [observed, *[lives[side] for side in sides], table]
    specs = [vmem, *[vmem for _ in sides], vmem]
    if stage != "first":
        args, specs = [received] + args, [vmem] + specs
    shapes, out_specs = [(PARTS, TILES + 1, 8, H)], [vmem]
    if stage == "last" and sides[0] == 1:
        shapes, out_specs = [(2, X, 8, H), (PARTS, TILES // 2, 8, H)], [vmem, vmem]
    elif stage == "last":
        shapes, out_specs = [(2, 2, X, 8, H)], [anywhere]
        scratch += [pltpu.VMEM((2, X, 8, H), F32), pltpu.SemaphoreType.DMA((16,))]
    outs = pl.pallas_call(
        functools.partial(lines_kernel, stage, sides),
        in_specs=[smem] + specs,
        out_specs=out_specs,
        out_shape=[jax.ShapeDtypeStruct(shape, F32) for shape in shapes],
        scratch_shapes=scratch,
        compiler_params=pltpu.CompilerParams(vmem_limit_bytes=18 * MIB),
        name="lines_" + stage,
    )(core, *args)
    return outs if len(outs) > 1 else outs[0]


def place_kernel(core_ref, got, rebuilt, out, sems):
    copies = []
    for comp in range(2):
        for part in range(8):
            rows = pl.ds(8 * part, 8)
            copies.append(
                pltpu.make_async_copy(
                    got.at[comp, rows], out.at[comp, 1 - core_ref[0], rows], sems.at[8 * comp + part]
                )
            )
    for copy in copies:
        copy.start()
    for copy in copies:
        copy.wait()


def place(core, got, rebuilt):
    anywhere = pl.BlockSpec(memory_space=pl.ANY)
    return pl.pallas_call(
        place_kernel,
        in_specs=[
            pl.BlockSpec(memory_space=pltpu.SMEM),
            pl.BlockSpec(memory_space=pltpu.VMEM),
            anywhere,
        ],
        out_specs=anywhere,
        out_shape=jax.ShapeDtypeStruct(rebuilt.shape, F32),
        scratch_shapes=[pltpu.SemaphoreType.DMA((16,))],
        input_output_aliases={2: 0},
        compiler_params=pltpu.CompilerParams(vmem_limit_bytes=8 * MIB),
        name="place",
    )(core, got, rebuilt)


def columns_kernel(tau, core_ref, received, forward, inverse, out):
    total = jnp.sum(received[:, TILES, :, :128]) * (1.0 / 1024.0)
    floor = tau * (total / CELLS) + 1e-06

    def column(kx, carry):
        tiles = []
        for k in range(8):
            for yt in range(2):
                for c in range(2):
                    tiles.append(received[k, yt * 16 + c * 8 + kx])
        high, low = split(jnp.concatenate(tiles, axis=0))
        both = dot(forward[...], high)
        value = both[:256] + both[256:] + dot(forward[:256], low)
        re, im = value[:128], value[128:]
        power = re * re + im * im
        gain = power / (power + floor)
        high, low = split(jnp.concatenate([re * gain, im * gain], axis=0))
        both = dot(inverse[...], high)
        value = both[:256] + both[256:] + dot(inverse[:256], low)
        row = 0
        for k in range(8):
            for yt in range(2):
                for c in range(2):
                    out[k, yt * 16 + c * 8 + kx] = value[row : row + 8]
                    row += 8
        return carry

    @pl.when(core_ref[0] == 0)
    def _():
        lax.fori_loop(0, 8, column, 0, unroll=8)

    @pl.when(core_ref[0] != 0)
    def _():
        lax.fori_loop(0, 8, column, 0, unroll=2)


def columns(tau, core, received, forward, inverse):
    vmem = pl.BlockSpec(memory_space=pltpu.VMEM)
    return pl.pallas_call(
        functools.partial(columns_kernel, tau),
        in_specs=[pl.BlockSpec(memory_space=pltpu.SMEM)] + [vmem] * 3,
        out_specs=vmem,
        out_shape=jax.ShapeDtypeStruct((PARTS, TILES, 8, H), F32),
        compiler_params=pltpu.CompilerParams(vmem_limit_bytes=16 * MIB),
        name="columns",
    )(core, received, forward, inverse)


def per_device(traces, live):
    core = lax.axis_index("c")[None]
    swap = [(0, 1), (1, 0)]
    lives = [live, lax.ppermute(live, "c", swap)]
    offsets = jnp.asarray(offset_tables())
    forward, inverse = (jnp.asarray(t) for t in cross_tables())

    joined, yours = temporal(core, traces, jnp.asarray(time_tables()))
    got = lax.ppermute(yours, "c", swap)
    ring = [(2 * x, (2 * x + 2) % 8) for x in range(4)]
    word = lax.ppermute(got[:2], ("x", "c"), ring)
    joined = join(joined, got, word, lives[1])
    observed = lax.all_to_all(joined, FREQ, 0, 0, tiled=True)

    both = (0, 1)
    message = lines("first", both, core, None, observed, lives, offsets)
    for step in range(ITERS):
        tau = 2.0 * 0.5**step
        whole = lax.all_to_all(message, SHARE, 0, 0, tiled=True)
        shrunk = columns(tau, core, whole, forward, inverse)
        back = lax.all_to_all(shrunk, SHARE, 0, 0, tiled=True)
        if step < ITERS - 1:
            message = lines("middle", both, core, back, observed, lives, offsets)
    yours, back = lines("last", (1,), core, back, observed, lives, offsets)
    got = lax.ppermute(yours, "c", swap)
    rebuilt = lines("last", (0,), core, back, observed, lives, offsets)
    return place(core, got, rebuilt)


def solution(mesh):
    inner = Mesh(mesh.devices.reshape(2, 4, 4, 2, 2), AXES)
    return jax.shard_map(
        per_device,
        mesh=inner,
        in_specs=(P(FREQ, SPACE, None, None), P(None, SPACE, None)),
        out_specs=P(None, FREQ, None, SPACE, None),
        check_vma=False,
    )
```

```python
import functools
import math

import jax
import jax.numpy as jnp
import ml_dtypes
import numpy as np
from jax import lax
from jax.experimental import pallas as pl
from jax.experimental.pallas import tpu as pltpu
from jax.sharding import Mesh, PartitionSpec as P

X = 64
Y = 128
HX = 16
HY = 16
H = 256
NT = 256
F = 16
ITERS = 3
CELLS = float(X * Y * H)
PARTS = 8
TILES = 32
MIB = 1 << 20

AXES = ("zh", "y", "x", "zl", "c")
FREQ = ("zh", "y")
SPACE = ("x", "zl", "c")
SHARE = ("x", "zl")
BF = jnp.bfloat16
F32 = jnp.float32


def split_np(table):
    high = table.astype(ml_dtypes.bfloat16)
    low = (table - high.astype(np.float64)).astype(ml_dtypes.bfloat16)
    return high, low


def block(matrix):
    return np.block([[matrix.real, matrix.imag], [-matrix.imag, matrix.real]])


def offset_tables():
    half = np.arange(HX // 2)
    cross = np.arange(HY)
    inline = np.exp(-2j * np.pi * np.outer(half, half) / (HX // 2))
    turned = np.exp(-2j * np.pi * half / HX)[:, None] * inline
    other = np.exp(-2j * np.pi * np.outer(cross, cross) / HY)
    even, odd = np.kron(inline, other), np.kron(turned, other)
    stack = []
    for matrix in (even, odd, odd.T):
        high, low = split_np(block(matrix) / math.sqrt(H * X))
        stack.append(np.concatenate([high, high, low], axis=0))
    return np.stack(stack)


def cross_tables():
    part, half, comp, cell = np.meshgrid(
        np.arange(8), np.arange(2), np.arange(2), np.arange(8), indexing="ij"
    )
    cells = (16 * part + 8 * half + cell).reshape(-1)
    comp = comp.reshape(-1)
    waves = np.arange(Y)
    angle = 2.0 * np.pi * (np.outer(waves, cells) % Y) / Y
    cosine, sine = np.cos(angle), np.sin(angle)
    real = np.where(comp == 0, cosine, sine)
    imag = np.where(comp == 0, -sine, cosine)
    forward = np.concatenate([real, imag], axis=0) / math.sqrt(Y)
    inverse = forward.T
    return np.concatenate(split_np(forward)), np.concatenate(split_np(inverse))


def split(value):
    high = value.astype(BF)
    low = (value - high.astype(F32)).astype(BF)
    return high, low


def three(left):
    high, low = split(left)
    return jnp.concatenate([high, low, high], axis=1)


def dot(left, right):
    return lax.dot_general(left, right, (((1,), (0,)), ((), ())), preferred_element_type=F32)


def time_kernel(core_ref, traces_hbm, joined, yours, traces, table, sems):
    copies = [
        pltpu.make_async_copy(traces_hbm.at[x], traces.at[x], sems.at[x]) for x in range(8)
    ]
    for copy in copies:
        copy.start()
    row = lax.broadcasted_iota(jnp.int32, (2 * F, NT), 0)
    time = lax.broadcasted_iota(jnp.int32, (2 * F, NT), 1)
    parity = jnp.where(row < F, core_ref[0], 1 - core_ref[0])
    turns = (time * ((row % F) // 2 * 2 + parity + 1)) % NT
    angle = turns.astype(F32) * (2.0 * math.pi / NT)
    values = jnp.where(row % 2 == 0, jnp.cos(angle), -jnp.sin(angle)) / math.sqrt(NT)
    table[: 2 * F], table[2 * F :] = split(values)
    dims = (((1,), (1,)), ((), ()))
    for x in range(8):
        copies[x].wait()
        rows = []
        for y in range(8):
            high, low = split(traces[x, y])
            both = lax.dot_general(table[...], high, dims, preferred_element_type=F32)
            rest = lax.dot_general(table[: 2 * F], low, dims, preferred_element_type=F32)
            rows.append(both[: 2 * F] + both[2 * F :] + rest)
        turned = jnp.swapaxes(jnp.stack(rows, axis=0), 0, 1)
        joined[:, 0, :, x] = turned[:F].reshape(8, 2, 8, H)
        yours[:, :, x] = turned[F:].reshape(8, 2, 8, H)


def temporal(core, traces):
    anywhere = pl.BlockSpec(memory_space=pl.ANY)
    return pl.pallas_call(
        time_kernel,
        in_specs=[pl.BlockSpec(memory_space=pltpu.SMEM), anywhere],
        out_specs=[pl.BlockSpec(memory_space=pltpu.VMEM)] * 2,
        out_shape=[
            jax.ShapeDtypeStruct((8, 2, 2, 8, 8, H), F32),
            jax.ShapeDtypeStruct((8, 2, 8, 8, H), F32),
        ],
        scratch_shapes=[
            pltpu.VMEM((8, 8, H, NT), F32),
            pltpu.VMEM((4 * F, NT), BF),
            pltpu.SemaphoreType.DMA((8,)),
        ],
        compiler_params=pltpu.CompilerParams(vmem_limit_bytes=50 * MIB),
        name="temporal",
    )(core, traces)


def join_kernel(joined, got, word, live, out):
    del joined, word, live
    out[:, 1] = got[...]


def join(joined, got, word, live):
    vmem = pl.BlockSpec(memory_space=pltpu.VMEM)
    anywhere = pl.BlockSpec(memory_space=pl.ANY)
    return pl.pallas_call(
        join_kernel,
        in_specs=[vmem] * 3 + [anywhere],
        out_specs=vmem,
        out_shape=jax.ShapeDtypeStruct(joined.shape, F32),
        input_output_aliases={0: 0},
        compiler_params=pltpu.CompilerParams(vmem_limit_bytes=8 * MIB),
        name="join",
    )(joined, got, word, live)


def add(a, b):
    return a[0] + b[0], a[1] + b[1]


def sub(a, b):
    return a[0] - b[0], a[1] - b[1]


def turn(a):
    return a[1], -a[0]


def four(a, b, c, d):
    s, t = add(a, c), sub(a, c)
    u, v = add(b, d), turn(sub(b, d))
    return add(s, u), add(t, v), sub(s, u), sub(t, v)


def eight(values):
    root = math.sqrt(0.5)
    e = four(values[0], values[2], values[4], values[6])
    o = four(values[1], values[3], values[5], values[7])
    o1 = ((o[1][0] + o[1][1]) * root, (o[1][1] - o[1][0]) * root)
    o2 = turn(o[2])
    o3 = ((o[3][1] - o[3][0]) * root, (-o[3][0] - o[3][1]) * root)
    odd = (o[0], o1, o2, o3)
    return [add(e[i], odd[i]) for i in range(4)] + [sub(e[i], odd[i]) for i in range(4)]


def twiddle(value, power):
    power %= 64
    if power == 0:
        return value
    cosine = math.cos(2.0 * math.pi * power / 64)
    sine = math.sin(2.0 * math.pi * power / 64)
    re, im = value
    return re * cosine + im * sine, im * cosine - re * sine


def lines_kernel(stage, sides, core_ref, *refs):
    refs = list(refs)
    first, last = stage == "first", stage == "last"
    received = None if first else refs.pop(0)
    observed = refs.pop(0)
    lives = [refs.pop(0) for _ in sides]
    table = refs.pop(0)
    out = refs.pop(0)
    ahead = last and sides[0] == 1
    kept_back = refs.pop(0) if ahead else None
    one, two = refs[:2]
    if last and not ahead:
        held, sent = refs[2:]
        whole, out = out, held
    lanes = [pl.ds(0, 128), pl.ds(128, 128)]
    power = jnp.zeros((8, 128), F32)

    for index, side in enumerate(sides):
        yt = core_ref[0] if side == 0 else 1 - core_ref[0]
        if not first:
            row = 0 if last and not ahead else yt * 16
            re = received[:, pl.ds(row, 8)].reshape(512, H)
            im = received[:, pl.ds(row + 8, 8)].reshape(512, H)
            even = dot(three(jnp.concatenate([im[:, :128], re[:, :128]], axis=1)), table[0])
            odd = dot(three(jnp.concatenate([im[:, 128:], re[:, 128:]], axis=1)), table[2])
            near, far = even + odd, even - odd
            for comp in range(2):
                cut = slice(128 * comp, 128 * comp + 128)
                one[comp, :, :, :, lanes[0]] = near[:, cut].reshape(8, 8, 8, 128)
                one[comp, :, :, :, lanes[1]] = far[:, cut].reshape(8, 8, 8, 128)
            for b in range(8):
                for lane in lanes:
                    values = eight([(one[0, a, b, :, lane], one[1, a, b, :, lane]) for a in range(8)])
                    for d in range(8):
                        re, im = twiddle(values[d], b * d)
                        two[0, d, b, :, lane] = re
                        two[1, d, b, :, lane] = im
        for d in range(8):
            for lane in lanes:
                seen = [
                    (observed[a, side, 0, d, :, lane], observed[a, side, 1, d, :, lane]) for a in range(8)
                ]
                kept = [lives[index][a * 8 + d, :, lane] > 0 for a in range(8)]
                if first:
                    back = [(0.0, 0.0)] * 8
                else:
                    back = eight([(two[0, d, b, :, lane], two[1, d, b, :, lane]) for b in range(8)])
                field = [
                    (jnp.where(kept[a], seen[a][0], back[a][1]), jnp.where(kept[a], seen[a][1], back[a][0]))
                    for a in range(8)
                ]
                if last:
                    for a in range(8):
                        out[0, a * 8 + d, :, lane] = field[a][0]
                        out[1, a * 8 + d, :, lane] = field[a][1]
                    continue
                for re, im in field:
                    power = power + (re * re + im * im)
                values = eight(field)
                for k in range(8):
                    re, im = twiddle(values[k], d * k)
                    one[0, k, d, :, lane] = re
                    one[1, k, d, :, lane] = im
        if last:
            continue
        for k in range(8):
            for lane in lanes:
                values = eight([(one[0, k, b, :, lane], one[1, k, b, :, lane]) for b in range(8)])
                for c in range(8):
                    two[0, c, k, :, lane] = values[c][0]
                    two[1, c, k, :, lane] = values[c][1]
        re = two[0].reshape(512, H)
        im = two[1].reshape(512, H)
        near = jnp.concatenate([re[:, :128] + re[:, 128:], im[:, :128] + im[:, 128:]], axis=1)
        far = jnp.concatenate([re[:, :128] - re[:, 128:], im[:, :128] - im[:, 128:]], axis=1)
        for lane, value in zip(lanes, (dot(three(near), table[0]), dot(three(far), table[1]))):
            out[:, pl.ds(yt * 16, 8), :, lane] = value[:, :128].reshape(8, 8, 8, 128)
            out[:, pl.ds(yt * 16 + 8, 8), :, lane] = value[:, 128:].reshape(8, 8, 8, 128)
    if ahead:
        kept_back[...] = received[:, pl.ds(core_ref[0] * 16, 16)]
    elif last:
        copies = []
        for comp in range(2):
            for part in range(8):
                rows = pl.ds(8 * part, 8)
                copies.append(
                    pltpu.make_async_copy(
                        held.at[comp, rows], whole.at[comp, core_ref[0], rows], sent.at[8 * comp + part]
                    )
                )
        for copy in copies:
            copy.start()
        for copy in copies:
            copy.wait()
    if not last:
        total = jnp.sum(power)
        out[:, TILES] = jnp.full((8, 8, H), total, F32)


def lines(stage, sides, core, received, observed, lives, table):
    vmem = pl.BlockSpec(memory_space=pltpu.VMEM)
    smem = pl.BlockSpec(memory_space=pltpu.SMEM)
    anywhere = pl.BlockSpec(memory_space=pl.ANY)
    scratch = [
        pltpu.VMEM((2, 8, 8, 8, H), F32),
        pltpu.VMEM((2, 8, 8, 8, H), F32),
    ]
    args = [observed, *[lives[side] for side in sides], table]
    specs = [vmem, *[vmem for _ in sides], vmem]
    if stage != "first":
        args, specs = [received] + args, [vmem] + specs
    shapes, out_specs = [(PARTS, TILES + 1, 8, H)], [vmem]
    if stage == "last" and sides[0] == 1:
        shapes, out_specs = [(2, X, 8, H), (PARTS, TILES // 2, 8, H)], [vmem, vmem]
    elif stage == "last":
        shapes, out_specs = [(2, 2, X, 8, H)], [anywhere]
        scratch += [pltpu.VMEM((2, X, 8, H), F32), pltpu.SemaphoreType.DMA((16,))]
    outs = pl.pallas_call(
        functools.partial(lines_kernel, stage, sides),
        in_specs=[smem] + specs,
        out_specs=out_specs,
        out_shape=[jax.ShapeDtypeStruct(shape, F32) for shape in shapes],
        scratch_shapes=scratch,
        compiler_params=pltpu.CompilerParams(vmem_limit_bytes=18 * MIB),
        name="lines_" + stage,
    )(core, *args)
    return outs if len(outs) > 1 else outs[0]


def place_kernel(core_ref, got, rebuilt, out, sems):
    copies = []
    for comp in range(2):
        for part in range(8):
            rows = pl.ds(8 * part, 8)
            copies.append(
                pltpu.make_async_copy(
                    got.at[comp, rows], out.at[comp, 1 - core_ref[0], rows], sems.at[8 * comp + part]
                )
            )
    for copy in copies:
        copy.start()
    for copy in copies:
        copy.wait()


def place(core, got, rebuilt):
    anywhere = pl.BlockSpec(memory_space=pl.ANY)
    return pl.pallas_call(
        place_kernel,
        in_specs=[
            pl.BlockSpec(memory_space=pltpu.SMEM),
            pl.BlockSpec(memory_space=pltpu.VMEM),
            anywhere,
        ],
        out_specs=anywhere,
        out_shape=jax.ShapeDtypeStruct(rebuilt.shape, F32),
        scratch_shapes=[pltpu.SemaphoreType.DMA((16,))],
        input_output_aliases={2: 0},
        compiler_params=pltpu.CompilerParams(vmem_limit_bytes=8 * MIB),
        name="place",
    )(core, got, rebuilt)


def columns_kernel(tau, core_ref, received, forward, inverse, out):
    total = jnp.sum(received[:, TILES, :, :128]) * (1.0 / 1024.0)
    floor = tau * (total / CELLS) + 1e-06

    def column(kx, carry):
        tiles = []
        for k in range(8):
            for yt in range(2):
                for c in range(2):
                    tiles.append(received[k, yt * 16 + c * 8 + kx])
        high, low = split(jnp.concatenate(tiles, axis=0))
        both = dot(forward[...], high)
        value = both[:256] + both[256:] + dot(forward[:256], low)
        re, im = value[:128], value[128:]
        power = re * re + im * im
        gain = power / (power + floor)
        high, low = split(jnp.concatenate([re * gain, im * gain], axis=0))
        both = dot(inverse[...], high)
        value = both[:256] + both[256:] + dot(inverse[:256], low)
        row = 0
        for k in range(8):
            for yt in range(2):
                for c in range(2):
                    out[k, yt * 16 + c * 8 + kx] = value[row : row + 8]
                    row += 8
        return carry

    @pl.when(core_ref[0] == 0)
    def _():
        lax.fori_loop(0, 8, column, 0, unroll=8)

    @pl.when(core_ref[0] != 0)
    def _():
        lax.fori_loop(0, 8, column, 0, unroll=2)


def columns(tau, core, received, forward, inverse):
    vmem = pl.BlockSpec(memory_space=pltpu.VMEM)
    return pl.pallas_call(
        functools.partial(columns_kernel, tau),
        in_specs=[pl.BlockSpec(memory_space=pltpu.SMEM)] + [vmem] * 3,
        out_specs=vmem,
        out_shape=jax.ShapeDtypeStruct((PARTS, TILES, 8, H), F32),
        compiler_params=pltpu.CompilerParams(vmem_limit_bytes=16 * MIB),
        name="columns",
    )(core, received, forward, inverse)


def per_device(traces, live):
    core = lax.axis_index("c")[None]
    swap = [(0, 1), (1, 0)]
    lives = [live, lax.ppermute(live, "c", swap)]
    offsets = jnp.asarray(offset_tables())
    forward, inverse = (jnp.asarray(t) for t in cross_tables())

    joined, yours = temporal(core, traces)
    got = lax.ppermute(yours, "c", swap)
    ring = [(2 * x, (2 * x + 2) % 8) for x in range(4)]
    word = lax.ppermute(got[:2], ("x", "c"), ring)
    joined = join(joined, got, word, lives[1])
    observed = lax.all_to_all(joined, FREQ, 0, 0, tiled=True)

    both = (0, 1)
    message = lines("first", both, core, None, observed, lives, offsets)
    for step in range(ITERS):
        tau = 2.0 * 0.5**step
        whole = lax.all_to_all(message, SHARE, 0, 0, tiled=True)
        shrunk = columns(tau, core, whole, forward, inverse)
        back = lax.all_to_all(shrunk, SHARE, 0, 0, tiled=True)
        if step < ITERS - 1:
            message = lines("middle", both, core, back, observed, lives, offsets)
    yours, back = lines("last", (1,), core, back, observed, lives, offsets)
    got = lax.ppermute(yours, "c", swap)
    rebuilt = lines("last", (0,), core, back, observed, lives, offsets)
    return place(core, got, rebuilt)


def solution(mesh):
    inner = Mesh(mesh.devices.reshape(2, 4, 4, 2, 2), AXES)
    return jax.shard_map(
        per_device,
        mesh=inner,
        in_specs=(P(FREQ, SPACE, None, None), P(None, SPACE, None)),
        out_specs=P(None, FREQ, None, SPACE, None),
        check_vma=False,
    )
```

```python
import functools
import math

import jax
import jax.numpy as jnp
import ml_dtypes
import numpy as np
from jax import lax
from jax.experimental import pallas as pl
from jax.experimental.pallas import tpu as pltpu
from jax.sharding import Mesh, PartitionSpec as P

X = 64
Y = 128
HX = 16
HY = 16
H = 256
NT = 256
F = 16
ITERS = 3
CELLS = float(X * Y * H)
PARTS = 8
TILES = 32
MIB = 1 << 20

AXES = ("zh", "y", "x", "zl", "c")
FREQ = ("zh", "y")
SPACE = ("x", "zl", "c")
SHARE = ("x", "zl")
BF = jnp.bfloat16
F32 = jnp.float32


def split_np(table):
    high = table.astype(ml_dtypes.bfloat16)
    low = (table - high.astype(np.float64)).astype(ml_dtypes.bfloat16)
    return high, low


def block(matrix):
    return np.block([[matrix.real, matrix.imag], [-matrix.imag, matrix.real]])


def offset_tables():
    half = np.arange(HX // 2)
    cross = np.arange(HY)
    inline = np.exp(-2j * np.pi * np.outer(half, half) / (HX // 2))
    turned = np.exp(-2j * np.pi * half / HX)[:, None] * inline
    other = np.exp(-2j * np.pi * np.outer(cross, cross) / HY)
    even, odd = np.kron(inline, other), np.kron(turned, other)
    stack = []
    for matrix in (even, odd, odd.T):
        high, low = split_np(block(matrix) / math.sqrt(H * X))
        stack.append(np.concatenate([high, high, low], axis=0))
    return np.stack(stack)


def cross_tables():
    part, half, comp, cell = np.meshgrid(
        np.arange(8), np.arange(2), np.arange(2), np.arange(8), indexing="ij"
    )
    cells = (16 * part + 8 * half + cell).reshape(-1)
    comp = comp.reshape(-1)
    waves = np.arange(Y)
    angle = 2.0 * np.pi * (np.outer(waves, cells) % Y) / Y
    cosine, sine = np.cos(angle), np.sin(angle)
    real = np.where(comp == 0, cosine, sine)
    imag = np.where(comp == 0, -sine, cosine)
    forward = np.concatenate([real, imag], axis=0) / math.sqrt(Y)
    inverse = forward.T
    return np.concatenate(split_np(forward)), np.concatenate(split_np(inverse))


def split(value):
    high = value.astype(BF)
    low = (value - high.astype(F32)).astype(BF)
    return high, low


def three(left):
    high, low = split(left)
    return jnp.concatenate([high, low, high], axis=1)


def dot(left, right):
    return lax.dot_general(left, right, (((1,), (0,)), ((), ())), preferred_element_type=F32)


def time_kernel(core_ref, traces_hbm, joined, yours, traces, table, sems):
    copies = [
        pltpu.make_async_copy(traces_hbm.at[x], traces.at[x], sems.at[x]) for x in range(8)
    ]
    for copy in copies:
        copy.start()
    row = lax.broadcasted_iota(jnp.int32, (2 * F, NT), 0)
    time = lax.broadcasted_iota(jnp.int32, (2 * F, NT), 1)
    parity = jnp.where(row < F, core_ref[0], 1 - core_ref[0])
    turns = (time * ((row % F) // 2 * 2 + parity + 1)) % NT
    angle = turns.astype(F32) * (2.0 * math.pi / NT)
    values = jnp.where(row % 2 == 0, jnp.cos(angle), -jnp.sin(angle)) / math.sqrt(NT)
    table[: 2 * F], table[2 * F :] = split(values)
    dims = (((1,), (1,)), ((), ()))
    for x in range(8):
        copies[x].wait()
        rows = []
        for y in range(8):
            high, low = split(traces[x, y])
            both = lax.dot_general(table[...], high, dims, preferred_element_type=F32)
            rest = lax.dot_general(table[: 2 * F], low, dims, preferred_element_type=F32)
            rows.append(both[: 2 * F] + both[2 * F :] + rest)
        turned = jnp.swapaxes(jnp.stack(rows, axis=0), 0, 1)
        joined[:, 0, :, x] = turned[:F].reshape(8, 2, 8, H)
        yours[:, :, x] = turned[F:].reshape(8, 2, 8, H)


def temporal(core, traces):
    anywhere = pl.BlockSpec(memory_space=pl.ANY)
    return pl.pallas_call(
        time_kernel,
        in_specs=[pl.BlockSpec(memory_space=pltpu.SMEM), anywhere],
        out_specs=[pl.BlockSpec(memory_space=pltpu.VMEM)] * 2,
        out_shape=[
            jax.ShapeDtypeStruct((8, 2, 2, 8, 8, H), F32),
            jax.ShapeDtypeStruct((8, 2, 8, 8, H), F32),
        ],
        scratch_shapes=[
            pltpu.VMEM((8, 8, H, NT), F32),
            pltpu.VMEM((4 * F, NT), BF),
            pltpu.SemaphoreType.DMA((8,)),
        ],
        compiler_params=pltpu.CompilerParams(vmem_limit_bytes=50 * MIB),
        name="temporal",
    )(core, traces)


def join_kernel(joined, got, word, live, out):
    del joined, word, live
    out[:, 1] = got[...]


def join(joined, got, word, live):
    vmem = pl.BlockSpec(memory_space=pltpu.VMEM)
    anywhere = pl.BlockSpec(memory_space=pl.ANY)
    return pl.pallas_call(
        join_kernel,
        in_specs=[vmem] * 3 + [anywhere],
        out_specs=vmem,
        out_shape=jax.ShapeDtypeStruct(joined.shape, F32),
        input_output_aliases={0: 0},
        compiler_params=pltpu.CompilerParams(vmem_limit_bytes=8 * MIB),
        name="join",
    )(joined, got, word, live)


def add(a, b):
    return a[0] + b[0], a[1] + b[1]


def sub(a, b):
    return a[0] - b[0], a[1] - b[1]


def turn(a):
    return a[1], -a[0]


def four(a, b, c, d):
    s, t = add(a, c), sub(a, c)
    u, v = add(b, d), turn(sub(b, d))
    return add(s, u), add(t, v), sub(s, u), sub(t, v)


def eight(values):
    root = math.sqrt(0.5)
    e = four(values[0], values[2], values[4], values[6])
    o = four(values[1], values[3], values[5], values[7])
    o1 = ((o[1][0] + o[1][1]) * root, (o[1][1] - o[1][0]) * root)
    o2 = turn(o[2])
    o3 = ((o[3][1] - o[3][0]) * root, (-o[3][0] - o[3][1]) * root)
    odd = (o[0], o1, o2, o3)
    return [add(e[i], odd[i]) for i in range(4)] + [sub(e[i], odd[i]) for i in range(4)]


def twiddle(value, power):
    power %= 64
    if power == 0:
        return value
    cosine = math.cos(2.0 * math.pi * power / 64)
    sine = math.sin(2.0 * math.pi * power / 64)
    re, im = value
    return re * cosine + im * sine, im * cosine - re * sine


def lines_kernel(stage, sides, core_ref, *refs):
    refs = list(refs)
    first, last = stage == "first", stage == "last"
    received = None if first else refs.pop(0)
    observed = refs.pop(0)
    lives = [refs.pop(0) for _ in sides]
    table = refs.pop(0)
    out = refs.pop(0)
    ahead = last and sides[0] == 1
    kept_back = refs.pop(0) if ahead else None
    one, two = refs[:2]
    if last and not ahead:
        held, sent = refs[2:]
        whole, out = out, held
    lanes = [pl.ds(0, 128), pl.ds(128, 128)]
    power = jnp.zeros((8, 128), F32)

    for index, side in enumerate(sides):
        yt = core_ref[0] if side == 0 else 1 - core_ref[0]
        if not first:
            row = 0 if last and not ahead else yt * 16
            re = received[:, pl.ds(row, 8)].reshape(512, H)
            im = received[:, pl.ds(row + 8, 8)].reshape(512, H)
            even = dot(three(jnp.concatenate([im[:, :128], re[:, :128]], axis=1)), table[0])
            odd = dot(three(jnp.concatenate([im[:, 128:], re[:, 128:]], axis=1)), table[2])
            near, far = even + odd, even - odd
            for comp in range(2):
                cut = slice(128 * comp, 128 * comp + 128)
                one[comp, :, :, :, lanes[0]] = near[:, cut].reshape(8, 8, 8, 128)
                one[comp, :, :, :, lanes[1]] = far[:, cut].reshape(8, 8, 8, 128)
            for b in range(8):
                for lane in lanes:
                    values = eight([(one[0, a, b, :, lane], one[1, a, b, :, lane]) for a in range(8)])
                    for d in range(8):
                        re, im = twiddle(values[d], b * d)
                        two[0, d, b, :, lane] = re
                        two[1, d, b, :, lane] = im
        for d in range(8):
            for lane in lanes:
                seen = [
                    (observed[a, side, 0, d, :, lane], observed[a, side, 1, d, :, lane]) for a in range(8)
                ]
                kept = [lives[index][a * 8 + d, :, lane] > 0 for a in range(8)]
                if first:
                    back = [(0.0, 0.0)] * 8
                else:
                    back = eight([(two[0, d, b, :, lane], two[1, d, b, :, lane]) for b in range(8)])
                field = [
                    (jnp.where(kept[a], seen[a][0], back[a][1]), jnp.where(kept[a], seen[a][1], back[a][0]))
                    for a in range(8)
                ]
                if last:
                    for a in range(8):
                        out[0, a * 8 + d, :, lane] = field[a][0]
                        out[1, a * 8 + d, :, lane] = field[a][1]
                    continue
                for re, im in field:
                    power = power + (re * re + im * im)
                values = eight(field)
                for k in range(8):
                    re, im = twiddle(values[k], d * k)
                    one[0, k, d, :, lane] = re
                    one[1, k, d, :, lane] = im
        if last:
            continue
        for k in range(8):
            for lane in lanes:
                values = eight([(one[0, k, b, :, lane], one[1, k, b, :, lane]) for b in range(8)])
                for c in range(8):
                    two[0, c, k, :, lane] = values[c][0]
                    two[1, c, k, :, lane] = values[c][1]
        re = two[0].reshape(512, H)
        im = two[1].reshape(512, H)
        near = jnp.concatenate([re[:, :128] + re[:, 128:], im[:, :128] + im[:, 128:]], axis=1)
        far = jnp.concatenate([re[:, :128] - re[:, 128:], im[:, :128] - im[:, 128:]], axis=1)
        for lane, value in zip(lanes, (dot(three(near), table[0]), dot(three(far), table[1]))):
            tile = lane.start // 128 * TILES + yt * 16
            out[:, pl.ds(tile, 8)] = value[:, :128].reshape(8, 8, 8, 128)
            out[:, pl.ds(tile + 8, 8)] = value[:, 128:].reshape(8, 8, 8, 128)
    if ahead:
        kept_back[...] = received[:, pl.ds(core_ref[0] * 16, 16)]
    elif last:
        copies = []
        for comp in range(2):
            for part in range(8):
                rows = pl.ds(8 * part, 8)
                copies.append(
                    pltpu.make_async_copy(
                        held.at[comp, rows], whole.at[comp, core_ref[0], rows], sent.at[8 * comp + part]
                    )
                )
        for copy in copies:
            copy.start()
        for copy in copies:
            copy.wait()
    if not last:
        total = jnp.sum(power)
        out[:, 2 * TILES] = jnp.full((8, 8, 128), total, F32)


def lines(stage, sides, core, received, observed, lives, table):
    vmem = pl.BlockSpec(memory_space=pltpu.VMEM)
    smem = pl.BlockSpec(memory_space=pltpu.SMEM)
    anywhere = pl.BlockSpec(memory_space=pl.ANY)
    scratch = [
        pltpu.VMEM((2, 8, 8, 8, H), F32),
        pltpu.VMEM((2, 8, 8, 8, H), F32),
    ]
    args = [observed, *[lives[side] for side in sides], table]
    specs = [vmem, *[vmem for _ in sides], vmem]
    if stage != "first":
        args, specs = [received] + args, [vmem] + specs
    shapes, out_specs = [(PARTS, 2 * TILES + 1, 8, 128)], [vmem]
    if stage == "last" and sides[0] == 1:
        shapes, out_specs = [(2, X, 8, H), (PARTS, TILES // 2, 8, H)], [vmem, vmem]
    elif stage == "last":
        shapes, out_specs = [(2, 2, X, 8, H)], [anywhere]
        scratch += [pltpu.VMEM((2, X, 8, H), F32), pltpu.SemaphoreType.DMA((16,))]
    outs = pl.pallas_call(
        functools.partial(lines_kernel, stage, sides),
        in_specs=[smem] + specs,
        out_specs=out_specs,
        out_shape=[jax.ShapeDtypeStruct(shape, F32) for shape in shapes],
        scratch_shapes=scratch,
        compiler_params=pltpu.CompilerParams(vmem_limit_bytes=18 * MIB),
        name="lines_" + stage,
    )(core, *args)
    return outs if len(outs) > 1 else outs[0]


def place_kernel(core_ref, got, rebuilt, out, sems):
    copies = []
    for comp in range(2):
        for part in range(8):
            rows = pl.ds(8 * part, 8)
            copies.append(
                pltpu.make_async_copy(
                    got.at[comp, rows], out.at[comp, 1 - core_ref[0], rows], sems.at[8 * comp + part]
                )
            )
    for copy in copies:
        copy.start()
    for copy in copies:
        copy.wait()


def place(core, got, rebuilt):
    anywhere = pl.BlockSpec(memory_space=pl.ANY)
    return pl.pallas_call(
        place_kernel,
        in_specs=[
            pl.BlockSpec(memory_space=pltpu.SMEM),
            pl.BlockSpec(memory_space=pltpu.VMEM),
            anywhere,
        ],
        out_specs=anywhere,
        out_shape=jax.ShapeDtypeStruct(rebuilt.shape, F32),
        scratch_shapes=[pltpu.SemaphoreType.DMA((16,))],
        input_output_aliases={2: 0},
        compiler_params=pltpu.CompilerParams(vmem_limit_bytes=8 * MIB),
        name="place",
    )(core, got, rebuilt)


def columns_kernel(tau, core_ref, received, forward, inverse, out):
    total = jnp.sum(received[:, 2 * TILES]) * (1.0 / 1024.0)
    floor = tau * (total / CELLS) + 1e-06

    def column(kx, carry):
        tiles = []
        for k in range(8):
            for yt in range(2):
                for c in range(2):
                    tile = yt * 16 + c * 8 + kx
                    halves = [received[k, tile], received[k, TILES + tile]]
                    tiles.append(jnp.concatenate(halves, axis=1))
        high, low = split(jnp.concatenate(tiles, axis=0))
        both = dot(forward[...], high)
        value = both[:256] + both[256:] + dot(forward[:256], low)
        re, im = value[:128], value[128:]
        power = re * re + im * im
        gain = power / (power + floor)
        high, low = split(jnp.concatenate([re * gain, im * gain], axis=0))
        both = dot(inverse[...], high)
        value = both[:256] + both[256:] + dot(inverse[:256], low)
        row = 0
        for k in range(8):
            for yt in range(2):
                for c in range(2):
                    out[k, yt * 16 + c * 8 + kx] = value[row : row + 8]
                    row += 8
        return carry

    @pl.when(core_ref[0] == 0)
    def _():
        lax.fori_loop(0, 8, column, 0, unroll=8)

    @pl.when(core_ref[0] != 0)
    def _():
        lax.fori_loop(0, 8, column, 0, unroll=2)


def columns(tau, core, received, forward, inverse):
    vmem = pl.BlockSpec(memory_space=pltpu.VMEM)
    return pl.pallas_call(
        functools.partial(columns_kernel, tau),
        in_specs=[pl.BlockSpec(memory_space=pltpu.SMEM)] + [vmem] * 3,
        out_specs=vmem,
        out_shape=jax.ShapeDtypeStruct((PARTS, TILES, 8, H), F32),
        compiler_params=pltpu.CompilerParams(vmem_limit_bytes=16 * MIB),
        name="columns",
    )(core, received, forward, inverse)


def per_device(traces, live):
    core = lax.axis_index("c")[None]
    swap = [(0, 1), (1, 0)]
    lives = [live, lax.ppermute(live, "c", swap)]
    offsets = jnp.asarray(offset_tables())
    forward, inverse = (jnp.asarray(t) for t in cross_tables())

    joined, yours = temporal(core, traces)
    got = lax.ppermute(yours, "c", swap)
    ring = [(2 * x, (2 * x + 2) % 8) for x in range(4)]
    word = lax.ppermute(got[:2], ("x", "c"), ring)
    joined = join(joined, got, word, lives[1])
    observed = lax.all_to_all(joined, FREQ, 0, 0, tiled=True)

    both = (0, 1)
    message = lines("first", both, core, None, observed, lives, offsets)
    for step in range(ITERS):
        tau = 2.0 * 0.5**step
        whole = lax.all_to_all(message, SHARE, 0, 0, tiled=True)
        shrunk = columns(tau, core, whole, forward, inverse)
        back = lax.all_to_all(shrunk, SHARE, 0, 0, tiled=True)
        if step < ITERS - 1:
            message = lines("middle", both, core, back, observed, lives, offsets)
    yours, back = lines("last", (1,), core, back, observed, lives, offsets)
    got = lax.ppermute(yours, "c", swap)
    rebuilt = lines("last", (0,), core, back, observed, lives, offsets)
    return place(core, got, rebuilt)


def solution(mesh):
    inner = Mesh(mesh.devices.reshape(2, 4, 4, 2, 2), AXES)
    return jax.shard_map(
        per_device,
        mesh=inner,
        in_specs=(P(FREQ, SPACE, None, None), P(None, SPACE, None)),
        out_specs=P(None, FREQ, None, SPACE, None),
        check_vma=False,
    )
```
